256 devices in a mesh: pair: 8 (over x, core), sec: 32 (over z, y).
Axes of the slice: x: 4, y: 4, z: 8, core: 2. Of those that a mesh axis runs over, the one named last changes fastest.
Arguments:
- psi_blocks: bfloat16 [384, 128, 128], P('sec'), may hold values from -1 to 1
- sector_rows: int32 [384], P('sec'), may hold values from 16 to 128, as said below
- left_ops: bfloat16 [384, 128, 128], P('pair'), may hold values from -0.5 to 0.5
- connect: int32 [384, 384], P('pair', 'sec'), may hold values from 0 to 383
- tile_order: int32 [96], replicated, may hold values from 0 to 95, each once
Outputs:
- rdm_tiles: float32 [768, 64, 128], P(('pair', 'sec'))
The draws below stay inside these ranges and needn't reach their ends.
Inputs may be any that keep to these rules, and one draw needn't show every extreme that they name: `sector_rows`: every value from 16 to 128; some sector has all 128 states live. `tile_order`: A permutation of the tiles of one group.
All inputs are finite; a program needn't handle non-finite values.
Results may differ from the reference program's by a relative error of at most 0.0029.
Values may be sent and summed in bfloat16 or wider, within the bound.
No kernel may reach another device: no remote copies, remote signals or barrier semaphores. Data moves between devices by JAX's collectives and lax.ppermute only.
A program may use at most 128 MiB of HBM per device.

```python
import jax
import jax.numpy as jnp
from jax import lax

B = 128
PAIRS = 384
SECTORS = 384
TROWS = 64
NT = 96
N_PAIR = 8


def draw_sector_rows(key, part):
    key = jax.random.fold_in(key, 7)
    first_key, second_key = jax.random.split(key)
    counts = jax.random.randint(first_key, (SECTORS,), B // 8, B + 1)
    chosen = jax.random.randint(second_key, (), 0, SECTORS)
    return jnp.where(jnp.arange(SECTORS) == chosen, B, counts).astype(jnp.int32)


def with_ends(result, stream_key, least, high):
    index_at = [jax.random.randint(jax.random.fold_in(stream_key, axis), (), 0, length) for axis, length in enumerate(result.shape)]
    longest = result.shape.index(max(result.shape))
    next_to = index_at[:longest] + [(index_at[longest] + 1) % result.shape[longest]] + index_at[longest + 1:]
    return result.at[tuple(index_at)].set(least).at[tuple(next_to)].set(high)


def level_of(key, shape, cuts, least, top_value):
    factor_of, own = 1.0, jax.random.fold_in(key, 6)
    for dim, blocks in cuts:
        steps = jnp.exp(jax.random.uniform(jax.random.fold_in(own, dim), (blocks,), jnp.float32, least / len(cuts), top_value / len(cuts)))
        factor_of = factor_of * jnp.repeat(steps, shape[dim] // blocks).reshape([-1 if axis == dim else 1 for axis in range(len(shape))])
    return factor_of


def bell_draw(rng, dims, deviation, bound, pieces=(), held_as=jnp.bfloat16):
    entries = deviation * jax.random.normal(rng, dims, jnp.float32)
    if pieces:
        entries = entries * level_of(rng, dims, pieces, -0.22, 0.18)
    return jnp.clip(entries, -bound, bound).astype(held_as)


def setup_inputs(seed: int = 0) -> dict:
    arg_keys = jax.random.split(jax.random.key(seed), 6)
    psi_blocks = bell_draw(arg_keys[0], (SECTORS, B, B), ((SECTORS * B) ** -0.25), 1.0, ((0, 32),))
    sector_rows = draw_sector_rows(jax.random.fold_in(arg_keys[5], 71), 0)
    left_ops = bell_draw(arg_keys[2], (PAIRS, B, B), B ** -0.5, 0.5, ((0, 8),))
    connect = with_ends(jax.random.randint(arg_keys[3], (PAIRS, SECTORS), 0, SECTORS), jax.random.fold_in(arg_keys[3], 1), 0, SECTORS - 1).astype(jnp.int32)
    tile_order = jax.random.permutation(arg_keys[4], NT).astype(jnp.int32)
    return {"psi_blocks": psi_blocks, "sector_rows": sector_rows, "left_ops": left_ops, "connect": connect, "tile_order": tile_order}


def reference(psi_blocks, sector_rows, left_ops, connect, tile_order):
    live_rows = jnp.arange(B)[None, :, None] < sector_rows[:, None, None]
    psi_live = jnp.where(live_rows, psi_blocks, jnp.zeros_like(psi_blocks))
    psi_wide = psi_live.astype(jnp.float32)

    def one_pair(inputs):
        operator, targets = inputs
        halves = jnp.einsum('sba,bc->sac', psi_wide, operator.astype(jnp.float32))
        halves = lax.optimization_barrier(halves.astype(jnp.bfloat16)).astype(jnp.float32)
        chosen = psi_wide[targets.astype(jnp.int32)]
        return jnp.einsum('sac,scd->ad', halves, chosen)

    density = lax.map(one_pair, (left_ops, connect))
    grouped = density.reshape(N_PAIR, NT, TROWS, B)
    coupled = grouped + jnp.roll(grouped, 1, axis=0)
    ordered = coupled[:, tile_order.astype(jnp.int32)]
    return ordered.reshape(N_PAIR * NT, TROWS, B)
```

```python
import functools

import jax
import jax.numpy as jnp
from jax import lax
from jax.experimental import pallas as pl
from jax.experimental.pallas import tpu as pltpu
from jax.sharding import PartitionSpec as P

NZ, NY = 8, 4
SLOTS = NZ * NY
SEC = 12
HALF = SEC // 2
R1, R2 = 48, 80
N1, N2 = HALF * R1, HALF * R2
NC = 16
TILES = 3
B = 128
F32, BF16 = jnp.float32, jnp.bfloat16


def zhop(v, d):
    route = [(z * NY + y, (z + d) % NZ * NY + y) for z in range(NZ) for y in range(NY)]
    return lax.ppermute(v, "sec", route)


def yhop(v, d):
    route = [(z * NY + y, z * NY + (y + d) % NY) for z in range(NZ) for y in range(NY)]
    return lax.ppermute(v, "sec", route)


def swap(v):
    return lax.ppermute(v, "pair", [(i, i ^ 1) for i in range(lax.axis_size("pair"))])


def gather_pieces(first, second):
    one, two = [], []
    left, right, over = yhop(first, 1), yhop(first, -1), yhop(first, 2)
    bundle = jnp.stack([first, left, right, over])
    dys = (0, -1, 1, 2)
    one.append((bundle, [(0, dy) for dy in dys], 1, 0))
    up = down = bundle
    zup = zdown = second
    groups = [[(second, 0)], [], []]
    for step in (1, 2, 3):
        zup, zdown = zhop(zup, 1), zhop(zdown, -1)
        groups[(0, 1, 2)[step - 1]] += [(zup, -step), (zdown, step)]
        up, down = zhop(up, 1), zhop(down, -1)
        one.append((up, [(-step, dy) for dy in dys], 1, 0))
        one.append((down, [(step, dy) for dy in dys], 1, 0))
    half = N2 // 2
    far = jnp.concatenate([zhop(zup[:half], 1), zhop(zdown[half:], -1)])
    groups[2].append((far, 4))
    one.append((zhop(up[:2], 1), [(4, dy) for dy in dys[:2]], 1, 0))
    one.append((zhop(down[2:], -1), [(4, dy) for dy in dys[2:]], 1, 0))
    for group in groups:
        block = jnp.stack([v for v, _ in group])
        dzs = [dz for _, dz in group]
        two.append((block, [(dz, 0) for dz in dzs], 2, 0))
        a, b = yhop(block, 1), yhop(block, -1)
        two.append((a, [(dz, -1) for dz in dzs], 2, 0))
        two.append((b, [(dz, 1) for dz in dzs], 2, 0))
        two.append((yhop(a[:, :half], 1), [(dz, 2) for dz in dzs], 2, 0))
        two.append((yhop(b[:, half:], -1), [(dz, 2) for dz in dzs], 2, half))
    return one, two


def tiles_kernel(plan, meta, conn, *refs):
    n = len(plan)
    pieces, ops, out = refs[:n], refs[n], refs[n + 1]
    ps1, ps2, turned, halves, weights, sems, opsem = refs[n + 2:]
    zpos, ypos, core = meta[TILES], meta[TILES + 1], meta[TILES + 2]

    def slot(dz, dy):
        return lax.rem(zpos + dz + NZ, NZ) * NY + lax.rem(ypos + dy + NY, NY)

    op_copies = [
        pltpu.make_async_copy(ops.at[meta[k] // 2], weights.at[k], opsem) for k in range(TILES)
    ]
    for copy in op_copies:
        copy.start()
    for ref, (slots, stream, row, rows, other) in zip(pieces, plan):
        home = (1 - core) if other else core
        for i, (dz, dy) in enumerate(slots):
            sem = sems.at[dz % NZ * NY + dy % NY]
            if stream == 1:
                dst = ps1.at[pl.ds((slot(dz, dy) * 2 + home) * N1, N1)]
                pltpu.make_async_copy(ref.at[i, pl.ds(0, N1)], dst, sem).start()
            else:
                dst = ps2.at[pl.ds((slot(dz, dy) * 2 + home) * N2 + row, rows)]
                pltpu.make_async_copy(ref.at[i], dst, sem).start()
    pltpu.make_async_copy(ops.at[pl.ds(0, TILES)], weights, opsem).wait()

    def sector(s):
        a = ps1[pl.ds(pl.multiple_of(s * R1, R1), R1), :]
        b = ps2[pl.ds(pl.multiple_of(s * R2, R2), R2), :]
        return jnp.concatenate([a, b], axis=0)

    def first_stage(j, carry):
        for u in range(2):
            r = j * 2 + u
            home = slot(r // NY, lax.rem(r, NY))
            whole1 = ps1.at[pl.ds(home * 2 * N1, 2 * N1)]
            whole2 = ps2.at[pl.ds(home * 2 * N2, 2 * N2)]
            pltpu.make_async_copy(whole1, whole1, sems.at[r]).wait()
            pltpu.make_async_copy(whole2, whole2, sems.at[r]).wait()
            for q in range(SEC):
                t = sector(home * SEC + q).T
                at, lanes = u * HALF + q // 2, pl.ds(q % 2 * B, B)
                turned[0, at, :, lanes] = t[:64]
                turned[1, at, :, lanes] = t[64:]
        for k in range(TILES):
            lhs = turned[lax.rem(meta[k], 2)]
            for e in range(2):
                part = lhs[:, :, e * B:(e + 1) * B].reshape(SEC * 64, B)
                r = jnp.dot(part, weights[k], preferred_element_type=F32).astype(BF16)
                halves[k, pl.ds(j * SEC, SEC), :, pl.ds(e * B, B)] = r.reshape(SEC, 64, B)
        return carry

    lax.fori_loop(0, SLOTS // 2, first_stage, 0)

    unroll = 16

    def second_stage(j, sums):
        sums = list(sums)
        for u in range(unroll):
            at = j * unroll + u
            for k in range(TILES):
                rhs = jnp.concatenate([sector(conn[k, 2 * at]), sector(conn[k, 2 * at + 1])], axis=0)
                sums[k] = sums[k] + jnp.dot(halves[k, at], rhs, preferred_element_type=F32)
        return tuple(sums)

    zero = jnp.zeros((64, B), F32)
    sums = lax.fori_loop(0, SLOTS * HALF // unroll, second_stage, (zero,) * TILES)
    for k in range(TILES):
        out[k] = sums[k]


def per_device(psi_blocks, sector_rows, left_ops, connect, tile_order):
    sec, pair = lax.axis_index("sec"), lax.axis_index("pair")
    zpos, ypos, core = sec // NY, sec % NY, pair % 2
    live = jnp.arange(B)[None, :, None] < sector_rows[:, None, None]
    psi_live = jnp.where(live, psi_blocks, jnp.zeros_like(psi_blocks))
    mine = lax.dynamic_slice_in_dim(psi_live, core * HALF, HALF, 0)
    both = jnp.stack([connect // 16, connect % 16], axis=-1).astype(BF16).reshape(-1)
    both = jnp.pad(both, (0, NC * B - both.size)).reshape(NC, B)
    first = jnp.concatenate([mine[:, :R1].reshape(N1, B), both])
    second = mine[:, R1:].reshape(N2, B)
    one, two = gather_pieces(first, second)

    pieces, plan = [], []
    for v, slots, stream, row in one + two:
        rows = N1 if stream == 1 else v.shape[1]
        for other in (False, True):
            pieces.append(swap(v) if other else v)
            plan.append((slots, stream, row, rows, other))

    found = {}
    for v, slots, _, _ in one:
        for i, (dz, dy) in enumerate(slots):
            found[dz % NZ * NY + dy % NY] = v[i, N1:]
    table = jnp.stack([found[r] for r in range(SLOTS)]).reshape(SLOTS, -1)[:, :connect.size * 2]
    table = table.reshape(SLOTS, connect.shape[0], SEC, 2)
    mytiles = lax.dynamic_slice_in_dim(tile_order, sec * TILES, TILES)
    table = jnp.take(table, mytiles // 2, axis=1).astype(jnp.int32)
    conn = (table[..., 0] * 16 + table[..., 1]).transpose(1, 0, 2).reshape(TILES, SLOTS * SEC)

    meta = jnp.concatenate([mytiles, jnp.stack([zpos, ypos, core]).astype(jnp.int32)])
    hbm = pl.BlockSpec(memory_space=pl.ANY)
    tiles = pl.pallas_call(
        functools.partial(tiles_kernel, plan),
        out_shape=jax.ShapeDtypeStruct((TILES, 64, B), F32),
        grid_spec=pltpu.PrefetchScalarGridSpec(
            num_scalar_prefetch=2,
            grid=(),
            in_specs=[hbm] * (len(pieces) + 1),
            out_specs=pl.BlockSpec(memory_space=pltpu.VMEM),
            scratch_shapes=[
                pltpu.VMEM((SLOTS * 2 * N1, B), BF16),
                pltpu.VMEM((SLOTS * 2 * N2, B), BF16),
                pltpu.VMEM((2, SEC, 64, 2 * B), BF16),
                pltpu.VMEM((TILES, SLOTS * HALF, 64, 2 * B), BF16),
                pltpu.VMEM((TILES, B, B), BF16),
                pltpu.SemaphoreType.DMA((SLOTS,)),
                pltpu.SemaphoreType.DMA,
            ],
        ),
        compiler_params=pltpu.CompilerParams(vmem_limit_bytes=48 * 2**20),
    )(meta, conn, *pieces, left_ops)
    ring = [((i - 1) % 8, i) for i in range(8)]
    return tiles + lax.ppermute(tiles, "pair", ring)


def solution(mesh):
    in_specs = (P("sec", None, None), P("sec"), P("pair", None, None), P("pair", "sec"), P())
    out_specs = P(("pair", "sec"), None, None)
    return jax.shard_map(
        per_device, mesh=mesh, in_specs=in_specs, out_specs=out_specs, check_vma=False
    )
```

```python
import functools

import jax
import jax.numpy as jnp
import numpy as np
from jax import lax
from jax.experimental import pallas as pl
from jax.experimental.pallas import tpu as pltpu
from jax.sharding import PartitionSpec as P

NZ, NY = 8, 4
SLOTS = NZ * NY
SEC = 12
B = 128
ROWS = SEC * B
S1 = 4
N1, N2 = S1 * B, (SEC - S1) * B
NC = 32
TILES = 3
VMEM_LIMIT = 60 * 2**20
F32, BF16 = jnp.float32, jnp.bfloat16


def hop(v, dz, dy):
    route = []
    for pair in range(8):
        s = -1 if pair % 2 else 1
        for z in range(NZ):
            for y in range(NY):
                to = (z + s * dz) % NZ * NY + (y + s * dy) % NY
                route.append((pair * SLOTS + z * NY + y, pair * SLOTS + to))
    return lax.ppermute(v, ("pair", "sec"), route)


def zhop(v):
    return hop(v, 1, 0)


def yhop(v):
    return hop(v, 0, 1)


def swap(v):
    return lax.ppermute(v, "pair", [(i, i ^ 1) for i in range(lax.axis_size("pair"))])


def part(v, core, axis=0):
    n = v.shape[axis] // 2
    return lax.dynamic_slice_in_dim(v, core * n, n, axis)


YS = (0, 1, 2, -1)


def sync(*arrays):
    return lax.optimization_barrier(arrays)


def gather_pieces(first, second, core, *others):
    n, h2 = first.shape[0], N2 // 2
    w1, near, far = zhop(second), yhop(first), hop(part(first, core), 0, 2)
    w1, near, far, *others = sync(w1, near, far, *others)

    w2, other, w1s = zhop(w1), swap(jnp.concatenate([near, far])), swap(w1)
    w2, other, w1s = sync(w2, other, w1s)

    near_s, far_s = other[:n], other[n:]
    far = jnp.where(core == 0, jnp.concatenate([far, far_s]), jnp.concatenate([far_s, far]))
    bundle = jnp.stack([first, near, far, near_s])
    own = jnp.where(core == 0, second, jnp.concatenate([second[h2:], second[:h2]]))
    a = jnp.concatenate([w1, own, w1s])
    bundle, a, w2 = sync(bundle, a, w2)
    w3, w4, z1, a1, w2s = zhop(w2), hop(part(w2, core), 2, 0), zhop(bundle), yhop(a), swap(w2)
    w3, w4, z1, a1, w2s = sync(w3, w4, z1, a1, w2s)

    ha = a.shape[0] // 2
    b = jnp.concatenate([w2, w2s])
    wc = jnp.concatenate([w3, w4])
    z2, a2, b1, wcs, a1s = zhop(z1), yhop(a1[:ha]), yhop(b), swap(wc), swap(a1)
    z2, a2, b1, wcs, a1s, wc = sync(z2, a2, b1, wcs, a1s, wc)

    c = jnp.concatenate([wc, wcs])
    hb, hc = b.shape[0] // 2, c.shape[0] // 2
    z3, c1, b2, z1s, a2s = zhop(z2), yhop(c), yhop(b1[:hb]), swap(z1), swap(a2)
    z3, c1, b2, z1s, a2s = sync(z3, c1, b2, z1s, a2s)

    z4, c2 = zhop(lax.dynamic_slice_in_dim(z3, core, 2, 0)), yhop(c1[:hc])
    z2s, b1s, c1s = swap(z2), swap(b1), swap(c1)
    z4, c2, z2s, b1s, c1s = sync(z4, c2, z2s, b1s, c1s)
    z3s, b2s, z4s, c2s = swap(z3), swap(b2), swap(z4), swap(c2)

    def step(dz):
        return [(i, dz, dy, 0) for i, dy in enumerate(YS)]

    def shift(seg, dy, stop):
        return [(r, m, dz, dy, o, e) for r, m, dz, _, o, e in seg if r < stop]

    a_seg = [(0, N2, 1, 0, 0, 0), (N2, h2, 0, 0, 0, h2), (N2 + h2, h2, 0, 0, h2, -h2),
             (2 * N2, N2, -1, 0, 0, 0)]
    b_seg = [(0, N2, 2, 0, 0, 0), (N2, N2, -2, 0, 0, 0)]
    c_seg = [(0, N2, 3, 0, 0, 0), (N2, h2, 4, 0, 0, h2), (hc, N2, -3, 0, 0, 0),
             (hc + N2, h2, 4, 0, h2, -h2)]
    corner = [(0, 4, 0, 1), (1, 4, 1, 1)]
    couples = [
        (2, c1, c1s, shift(c_seg, 1, 2 * hc)), (1, z3, z3s, step(3)), (2, b2, b2s, shift(b_seg, 2, hb)),
        (2, c2, c2s, shift(c_seg, 2, hc)), (1, z4, z4s, corner),
        (1, bundle, None, step(0)), (2, a, None, a_seg), (2, a1, a1s, shift(a_seg, 1, 2 * ha)),
        (1, z1, z1s, step(1)), (2, b, None, b_seg), (2, c, None, c_seg),
        (2, a2, a2s, shift(a_seg, 2, ha)), (2, b1, b1s, shift(b_seg, 1, 2 * hb)), (1, z2, z2s, step(2)),
    ]
    return couples, others


def place(seg, stream, core, swapped):
    who = 1 - core if swapped else core
    sign = 2 * who - 1
    if stream == 1:
        i, dz, dy, special = seg
        return dz * sign, (1 + i if who else -i) if special else dy * sign, 0, N1
    r, rows, dz, dy, o, more = seg
    return dz * sign, dy * sign, N1 + o + more * who, rows


def sectors(seg, stream, core, swapped):
    dz, dy, row, rows = place(seg, stream, core, swapped)
    return [(dz % NZ, dy % NY, row // B + q) for q in range(rows // B)]


def couple_order(couple, core):
    stream, _, v, segments = couple
    left = [t for seg in segments for t in sectors(seg, stream, core, False)]
    if v is None:
        half = len(left) // 2
        return list(zip(left[:half], left[half:]))
    return list(zip(left, [t for seg in segments for t in sectors(seg, stream, core, True)]))


def arrays_of(couples):
    return [(w, seg, st, swapped) for st, u, v, seg in couples
            for w, swapped in ((u, False), (v, True)) if w is not None]


def orders(couples):
    slots, pairs = [], []
    for core in (0, 1):
        rows = [place(t, 1, core, swapped)[:2] for _, seg, st, swapped in arrays_of(couples) if st == 1
                for t in seg]
        slots.append([(dz % NZ, dy % NY) for dz, dy in rows])
        pairs.append([p for couple in couples for p in couple_order(couple, core)])
    return slots, pairs


def couple_spec(couple):
    stream, u, v, _ = couple
    rows = u.shape[0] * N1 if stream == 1 else u.shape[0]
    count = rows // B // (2 if v is None else 1)
    return count, next(n for n in (12, 16, 8) if count % n == 0)


def prepare_kernel(rows, psi, here, there, first, second):
    core = lax.rem(lax.axis_index("pair"), 2)
    row = lax.broadcasted_iota(jnp.int32, (B, B), 0)
    for s in range(SEC):
        live = jnp.where(row < rows[s], psi[s], jnp.zeros((B, B), BF16))
        if s < S1:
            first[pl.ds(s * B, B), :] = live
        else:
            second[pl.ds((s - S1) * B, B), :] = live
    pairs = here.shape[0]
    lane = lax.broadcasted_iota(jnp.int32, (pairs, B), 1)
    pair = lax.broadcasted_iota(jnp.int32, (pairs, B), 0)
    high = jnp.where(lane == pair, 1.0, 0.0).astype(BF16)
    low = jnp.where(lane == pair + B // 2, 1.0, 0.0).astype(BF16)

    def words(ref):
        v = ref[...]
        contract = (((0,), (0,)), ((), ()))
        up = (v // 16).astype(F32).astype(BF16)
        down = (v % 16).astype(F32).astype(BF16)
        return (lax.dot_general(up, high, contract, preferred_element_type=F32)
                + lax.dot_general(down, low, contract, preferred_element_type=F32)).astype(BF16)

    mine, other = words(here), words(there)
    zero = jnp.zeros((16 - SEC, B), BF16)
    even = jnp.where(core == 0, mine, other)
    odd = jnp.where(core == 0, other, mine)
    first[pl.ds(N1, NC), :] = jnp.concatenate([even, zero, odd, zero], axis=0)


def tiles_kernel(specs, plan, meta, *refs):
    n = len(plan)
    pieces, ops, pick, out = refs[:n], *refs[n:n + 3]
    psi, halves, turned, words, table, conn, weights, sems, csem, osem = refs[n + 3:]
    core, zpos, ypos = meta[TILES], meta[TILES + 1], meta[TILES + 2]
    pairs = SLOTS * SEC // 2
    targets, places = TILES + 3, TILES + 3 + 2 * pairs

    for k in range(TILES):
        pltpu.make_async_copy(ops.at[meta[k] // 2], weights.at[k], osem).start()
    start = 0
    for ref, (segments, stream, swapped, couple) in zip(pieces, plan):
        if stream == 1:
            at = pl.ds(pl.multiple_of(N1 + core * 16, 16), 16)
            size = len(segments)
            pltpu.make_async_copy(ref.at[:, at], words.at[pl.ds(start, size)], csem).start()
            start += size
    for ref, (segments, stream, swapped, couple) in zip(pieces, plan):
        at_core = [[place(seg, stream, c, swapped) for seg in segments] for c in (0, 1)]
        for seg, (dz0, dy0, row0, rows), (dz1, dy1, row1, _) in zip(segments, *at_core):
            dz, dy = jnp.where(core == 0, dz0, dz1), jnp.where(core == 0, dy0, dy1)
            slot = lax.rem(zpos + dz + NZ, NZ) * NY + lax.rem(ypos + dy + NY, NY)
            row = slot * ROWS + jnp.where(core == 0, row0, row1)
            src = ref.at[seg[0], pl.ds(0, N1)] if stream == 1 else ref.at[pl.ds(seg[0], rows)]
            dst = psi.at[pl.ds(pl.multiple_of(row, B), rows)]
            pltpu.make_async_copy(src, dst, sems.at[couple]).start()
    pltpu.make_async_copy(ops.at[pl.ds(0, TILES)], weights, osem).wait()

    def sector(s):
        return psi[pl.ds(pl.multiple_of(s * B, B), B), :]

    base = 0
    for couple, (count, batch) in enumerate(specs):
        rows = psi.at[pl.ds(0, 2 * count * B)]
        pltpu.make_async_copy(rows, rows, sems.at[couple]).wait()

        def some(j, carry, batch=batch, base=base):
            for q in range(batch):
                for e in range(2):
                    t = sector(meta[places + 2 * (base + j * batch + q) + e]).T
                    for k in range(TILES):
                        low = lax.rem(meta[k], 2) == 0
                        turned[k, q, :, pl.ds(e * B, B)] = jnp.where(low, t[:64], t[64:])
            for k in range(TILES):
                for e in range(2):
                    rows = turned[k, pl.ds(0, batch), :, pl.ds(e * B, B)].reshape(batch * 64, B)
                    r = jnp.dot(rows, weights[k], preferred_element_type=F32).astype(BF16)
                    to = pl.ds(base + j * batch, batch)
                    halves[k, to, :, pl.ds(e * B, B)] = r.reshape(batch, 64, B)
            return carry

        lax.fori_loop(0, count // batch, some, 0)
        base += count
        if couple == 4:
            pltpu.make_async_copy(words, words, csem).wait()
            values = lax.dot_general(pick[...], words[...].reshape(SLOTS * 16, B), (((1,), (1,)), ((), ())),
            preferred_element_type=F32)
            table[...] = values.astype(jnp.int32)
            pltpu.make_async_copy(table, conn, csem).start()
    pltpu.make_async_copy(table, conn, csem).wait()

    unroll = 12

    def second_stage(j, sums):
        sums = list(sums)
        for u in range(unroll):
            at = j * unroll + u
            for k in range(TILES):
                left, right = (conn[k, meta[targets + 2 * at + e]] for e in (0, 1))
                rhs = jnp.concatenate([sector(left), sector(right)], axis=0)
                sums[k] = sums[k] + jnp.dot(halves[k, at], rhs, preferred_element_type=F32)
        return tuple(sums)

    sums = lax.fori_loop(0, pairs // unroll, second_stage, (jnp.zeros((64, B), F32),) * TILES)
    for k in range(TILES):
        out[k] = sums[k]


def tables():
    shapes = []

    def trace(first, second):
        couples, _ = gather_pieces(first, second, jnp.int32(0))
        shapes.extend(couples)
        return first

    jax.eval_shape(
        trace, jax.ShapeDtypeStruct((N1 + NC, B), BF16), jax.ShapeDtypeStruct((N2, B), BF16))
    slots, pairs = orders(shapes)
    index, places = [], []
    for c in (0, 1):
        number = {at: o for o, at in enumerate(slots[c])}
        flat = [t for p in pairs[c] for t in p]
        index.append([number[t[:2]] * 16 + t[2] for t in flat])
        places.append(flat)
    return np.array(index, np.int32), np.array(places, np.int32)


def per_device(psi_blocks, sector_rows, left_ops, connect, tile_order):
    sec, pair = lax.axis_index("sec"), lax.axis_index("pair")
    zpos, ypos, core = sec // NY, sec % NY, pair % 2
    vmem = pl.BlockSpec(memory_space=pltpu.VMEM)
    first, second = pl.pallas_call(
        prepare_kernel,
        out_shape=(jax.ShapeDtypeStruct((N1 + NC, B), BF16), jax.ShapeDtypeStruct((N2, B), BF16)),
        grid_spec=pltpu.PrefetchScalarGridSpec(
            num_scalar_prefetch=1, grid=(), in_specs=[vmem] * 3, out_specs=[vmem] * 2,
        ),
    )(sector_rows, psi_blocks, connect, swap(connect))

    mytiles = lax.dynamic_slice_in_dim(tile_order, sec * TILES, TILES)
    lane = jnp.arange(B)[None, :]
    mypairs = jnp.pad(mytiles // 2, (0, 16 - TILES))[:, None]
    pick = jnp.where(lane == mypairs, 16.0, 0.0) + jnp.where(lane == B // 2 + mypairs, 1.0, 0.0)
    pick = pick.astype(BF16)

    index, places = tables()
    index = jnp.asarray(index)[core]
    places = jnp.asarray(places)[core]
    places = ((zpos + places[:, 0]) % NZ * NY + (ypos + places[:, 1]) % NY) * SEC + places[:, 2]
    meta = jnp.concatenate([mytiles, jnp.stack([core, zpos, ypos]), index, places]).astype(jnp.int32)
    couples, (meta, pick) = gather_pieces(first, second, core, meta, pick)

    arrays = arrays_of(couples)
    plan = [(seg, st, swapped, number) for number, couple in enumerate(couples)
            for _, seg, st, swapped in arrays_of([couple])]
    hbm = pl.BlockSpec(memory_space=pl.ANY)
    tiles = pl.pallas_call(
        functools.partial(tiles_kernel, [couple_spec(couple) for couple in couples], plan),
        out_shape=jax.ShapeDtypeStruct((TILES, 64, B), F32),
        grid_spec=pltpu.PrefetchScalarGridSpec(
            num_scalar_prefetch=1,
            grid=(),
            in_specs=[hbm] * (len(plan) + 1) + [vmem],
            out_specs=vmem,
            scratch_shapes=[
                pltpu.VMEM((SLOTS * ROWS, B), BF16),
                pltpu.VMEM((TILES, SLOTS * SEC // 2, 64, 2 * B), BF16),
                pltpu.VMEM((TILES, 16, 64, 2 * B), BF16),
                pltpu.VMEM((SLOTS, 16, B), BF16),
                pltpu.VMEM((16, SLOTS * 16), jnp.int32),
                pltpu.SMEM((16, SLOTS * 16), jnp.int32),
                pltpu.VMEM((TILES, B, B), BF16),
                pltpu.SemaphoreType.DMA((len(couples),)),
                pltpu.SemaphoreType.DMA,
                pltpu.SemaphoreType.DMA,
            ],
        ),
        compiler_params=pltpu.CompilerParams(vmem_limit_bytes=VMEM_LIMIT),
    )(meta, *[w for w, _, _, _ in arrays], left_ops, pick)
    ring = [((i - 1) % 8, i) for i in range(8)]
    return tiles + lax.ppermute(tiles, "pair", ring)


def solution(mesh):
    in_specs = (P("sec", None, None), P("sec"), P("pair", None, None), P("pair", "sec"), P())
    out_specs = P(("pair", "sec"), None, None)
    return jax.shard_map(
        per_device, mesh=mesh, in_specs=in_specs, out_specs=out_specs, check_vma=False
    )
```

```python
import functools

import jax
import jax.numpy as jnp
import numpy as np
from jax import lax
from jax.experimental import pallas as pl
from jax.experimental.pallas import tpu as pltpu
from jax.sharding import PartitionSpec as P

NZ, NY = 8, 4
SLOTS = NZ * NY
SEC = 12
B = 128
ROWS = SEC * B
S1 = 4
N1, N2 = S1 * B, (SEC - S1) * B
NC = 32
TILES = 3
VMEM_LIMIT = 60 * 2**20
AHEAD = 2
F32, BF16 = jnp.float32, jnp.bfloat16


def hop(v, dz, dy):
    route = []
    for pair in range(8):
        s = -1 if pair % 2 else 1
        for z in range(NZ):
            for y in range(NY):
                to = (z + s * dz) % NZ * NY + (y + s * dy) % NY
                route.append((pair * SLOTS + z * NY + y, pair * SLOTS + to))
    return lax.ppermute(v, ("pair", "sec"), route)


def zhop(v):
    return hop(v, 1, 0)


def yhop(v):
    return hop(v, 0, 1)


def swap(v):
    return lax.ppermute(v, "pair", [(i, i ^ 1) for i in range(lax.axis_size("pair"))])


def part(v, core, axis=0):
    n = v.shape[axis] // 2
    return lax.dynamic_slice_in_dim(v, core * n, n, axis)


YS = (0, 1, 2, -1)


def sync(*arrays):
    return lax.optimization_barrier(arrays)


def gather_pieces(first, second, core, *others):
    n, h2 = first.shape[0], N2 // 2
    w1, near, far = zhop(second), yhop(first), hop(part(first, core), 0, 2)
    w1, near, far, *others = sync(w1, near, far, *others)

    w2, other = zhop(w1), swap(jnp.concatenate([near, far, w1]))
    w2, other = sync(w2, other)

    near_s, far_s, w1s = other[:n], other[n:n + n // 2], other[n + n // 2:]
    far = jnp.where(core == 0, jnp.concatenate([far, far_s]), jnp.concatenate([far_s, far]))
    bundle = jnp.concatenate([first, near, far, near_s])
    own = jnp.where(core == 0, second, jnp.concatenate([second[h2:], second[:h2]]))
    a = jnp.concatenate([w1, own, w1s])
    w3, z1, a1 = zhop(w2), zhop(bundle), yhop(a)
    w4, w2s = hop(part(w2, core), 2, 0), swap(w2)
    w3, z1, a1, w4, w2s = sync(w3, z1, a1, w4, w2s)

    ha = a.shape[0] // 2
    b = jnp.concatenate([w2, w2s])
    wc = jnp.concatenate([w3, w4])
    z2, ab, wcs, a1s = zhop(z1), yhop(jnp.concatenate([a1[:ha], b])), swap(wc), swap(a1)
    z2, ab, wcs, a1s = sync(z2, ab, wcs, a1s)

    c = jnp.concatenate([wc, wcs])
    hb, hc = b.shape[0] // 2, c.shape[0] // 2
    z3, cb, z1s, abs_ = zhop(z2), yhop(jnp.concatenate([c, ab[ha:ha + hb]])), swap(z1), swap(ab)
    z3, cb, z1s, abs_ = sync(z3, cb, z1s, abs_)

    z4, c2 = zhop(lax.dynamic_slice_in_dim(z3, core * n, 2 * n, 0)), yhop(cb[:hc])
    z2s, z3s, cbs = swap(z2), swap(z3), swap(cb)
    z4, c2, z2s, z3s, cbs = sync(z4, c2, z2s, z3s, cbs)
    z4s, c2s = swap(z4), swap(c2)

    def step(dz):
        return [(i * n, N1, dz, dy, 0, 0, False) for i, dy in enumerate(YS)]

    def shift(seg, dy, stop, by=0):
        return [(r + by, m, dz, dy, o, e, x) for r, m, dz, _, o, e, x in seg if r < stop]

    def rest(parts):
        segs, r = [], 0
        for rows, dz, o, more in parts:
            segs.append((r, rows, dz, 0, N1 + o, more, False))
            r += rows
        return segs

    a_seg = rest([(N2, 1, 0, 0), (h2, 0, 0, h2), (h2, 0, h2, -h2), (N2, -1, 0, 0)])
    b_seg = rest([(N2, 2, 0, 0), (N2, -2, 0, 0)])
    c_seg = rest([(N2, 3, 0, 0), (h2, 4, 0, h2), (N2, -3, 0, 0), (h2, 4, h2, -h2)])
    couples = [
        (bundle, None, step(0)), (a, None, a_seg), (a1, a1s, shift(a_seg, 1, 2 * ha)),
        (z1, z1s, step(1)), (b, None, b_seg), (c, None, c_seg),
        (ab, abs_, shift(a_seg, 2, ha) + shift(b_seg, 1, 2 * hb, ha)), (z2, z2s, step(2)),
        (cb, cbs, shift(c_seg, 1, 2 * hc) + shift(b_seg, 2, hb, 2 * hc)), (z3, z3s, step(3)),
        (c2, c2s, shift(c_seg, 2, hc)),
        (z4, z4s, [(i * n, N1, 4, i, 0, 0, True) for i in range(2)]),
    ]
    return couples, others


def place(seg, core, swapped):
    who = 1 - core if swapped else core
    sign = 2 * who - 1
    _, _, dz, dy, row, more, last = seg
    return dz * sign, (1 + dy if who else -dy) if last else dy * sign, row + more * who


def sectors(segments, core, swapped):
    found = []
    for seg in segments:
        dz, dy, row = place(seg, core, swapped)
        found += [(dz % NZ, dy % NY, row // B + q) for q in range(seg[1] // B)]
    return found


def arrays_of(couples):
    return [(w, seg, swapped, number) for number, (u, v, seg) in enumerate(couples)
            for w, swapped in ((u, False), (v, True)) if w is not None]


def couple_spec(couple):
    _, v, segments = couple
    count = sum(seg[1] for seg in segments) // B // (2 if v is None else 1)
    return count, next(n for n in (12, 16, 14, 8) if count % n == 0)


def tables():
    shapes = []

    def trace(first, second):
        couples, _ = gather_pieces(first, second, jnp.int32(0))
        shapes.extend(couples)
        return first

    jax.eval_shape(
        trace, jax.ShapeDtypeStruct((N1 + NC, B), BF16), jax.ShapeDtypeStruct((N2, B), BF16))
    index, places, segs = [], [], []
    for core in (0, 1):
        at = [(place(seg, core, swapped), seg[1]) for _, segments, swapped, _ in arrays_of(shapes)
              for seg in segments]
        number = {}
        for (dz, dy, row), rows in at:
            if row < N1:
                number[dz % NZ, dy % NY] = len(number)
        flat = []
        for _, v, segments in shapes:
            left = sectors(segments, core, False)
            half = len(left) // 2
            left, right = (left[:half], left[half:]) if v is None else (left, sectors(segments, core, True))
            flat += [t for p in zip(left, right) for t in p]
        index.append([number[t[:2]] * 16 + t[2] for t in flat])
        places.append(flat)
        segs.append([p for p, _ in at])
    return (np.array(t, np.int32) for t in (index, places, segs))


def prepare_kernel(rows, psi, here, there, first, second):
    core = lax.rem(lax.axis_index("pair"), 2)
    row = lax.broadcasted_iota(jnp.int32, (B, B), 0)
    for s in range(SEC):
        live = jnp.where(row < rows[s], psi[s], jnp.zeros((B, B), BF16))
        if s < S1:
            first[pl.ds(s * B, B), :] = live
        else:
            second[pl.ds((s - S1) * B, B), :] = live
    pairs = here.shape[0]
    lane = lax.broadcasted_iota(jnp.int32, (pairs, B), 1)
    pair = lax.broadcasted_iota(jnp.int32, (pairs, B), 0)
    high = jnp.where(lane == pair, 1.0, 0.0).astype(BF16)
    low = jnp.where(lane == pair + B // 2, 1.0, 0.0).astype(BF16)

    def words(ref):
        v = ref[...]
        contract = (((0,), (0,)), ((), ()))
        up = (v // 16).astype(F32).astype(BF16)
        down = (v % 16).astype(F32).astype(BF16)
        return (lax.dot_general(up, high, contract, preferred_element_type=F32)
                + lax.dot_general(down, low, contract, preferred_element_type=F32)).astype(BF16)

    mine, other = words(here), words(there)
    zero = jnp.zeros((16 - SEC, B), BF16)
    even = jnp.where(core == 0, mine, other)
    odd = jnp.where(core == 0, other, mine)
    first[pl.ds(N1, NC), :] = jnp.concatenate([even, zero, odd, zero], axis=0)


def tiles_kernel(specs, plan, meta, *refs):
    n = len(plan)
    pieces, ops, pick, out = refs[:n], *refs[n:n + 3]
    psi, halves, turned, words, table, conn, sems, csem = refs[n + 3:]
    core = meta[TILES]
    pairs = SLOTS * SEC // 2
    targets, places, rows_to = TILES + 1, TILES + 1 + 2 * pairs, TILES + 1 + 4 * pairs

    def fetch(wanted):
        number = 0
        for ref, (segments, couple) in zip(pieces, plan):
            for r, rows, _, _, row, _, _ in segments:
                if couple == wanted:
                    to = pl.ds(pl.multiple_of(meta[rows_to + number], B), rows)
                    pltpu.make_async_copy(ref.at[pl.ds(r, rows)], psi.at[to], sems.at[couple]).start()
                number += 1

    for couple in range(AHEAD):
        fetch(couple)
    slot = 0
    for ref, (segments, couple) in zip(pieces, plan):
        for r, rows, _, _, row, _, _ in segments:
            if row < N1:
                at = pl.ds(pl.multiple_of(r + N1 + core * 16, 16), 16)
                pltpu.make_async_copy(ref.at[at], words.at[slot], csem).start()
                slot += 1

    def sector(s):
        return psi[pl.ds(pl.multiple_of(s * B, B), B), :]

    base = 0
    for couple, (count, batch) in enumerate(specs):
        fetch(couple + AHEAD)
        rows = psi.at[pl.ds(0, 2 * count * B)]
        pltpu.make_async_copy(rows, rows, sems.at[couple]).wait()

        def some(j, carry, batch=batch, base=base):
            for q in range(batch):
                for e in range(2):
                    t = sector(meta[places + 2 * (base + j * batch + q) + e]).T
                    for k in range(TILES):
                        low = lax.rem(meta[k], 2) == 0
                        turned[k, q, :, pl.ds(e * B, B)] = jnp.where(low, t[:64], t[64:])
            for k in range(TILES):
                for e in range(2):
                    rows = turned[k, pl.ds(0, batch), :, pl.ds(e * B, B)].reshape(batch * 64, B)
                    r = jnp.dot(rows, ops[k], preferred_element_type=F32).astype(BF16)
                    to = pl.ds(base + j * batch, batch)
                    halves[k, to, :, pl.ds(e * B, B)] = r.reshape(batch, 64, B)
            return carry

        lax.fori_loop(0, count // batch, some, 0)
        base += count
        if couple == 6:
            pltpu.make_async_copy(words, words, csem).wait()
            values = lax.dot_general(pick[...], words[...].reshape(SLOTS * 16, B), (((1,), (1,)), ((), ())),
            preferred_element_type=F32)
            table[...] = values.astype(jnp.int32)
            pltpu.make_async_copy(table, conn, csem).start()
    pltpu.make_async_copy(table, conn, csem).wait()

    unroll = 48

    def second_stage(j, sums):
        sums = list(sums)
        for u in range(unroll):
            at = j * unroll + u
            for k in range(TILES):
                left, right = (conn[k, meta[targets + 2 * at + e]] for e in (0, 1))
                rhs = jnp.concatenate([sector(left), sector(right)], axis=0)
                sums[k] = sums[k] + jnp.dot(halves[k, at], rhs, preferred_element_type=F32)
        return tuple(sums)

    sums = lax.fori_loop(0, pairs // unroll, second_stage, (jnp.zeros((64, B), F32),) * TILES)
    for k in range(TILES):
        out[k] = sums[k]


def per_device(psi_blocks, sector_rows, left_ops, connect, tile_order):
    sec, pair = lax.axis_index("sec"), lax.axis_index("pair")
    zpos, ypos, core = sec // NY, sec % NY, pair % 2
    vmem = pl.BlockSpec(memory_space=pltpu.VMEM)
    first, second = pl.pallas_call(
        prepare_kernel,
        out_shape=(jax.ShapeDtypeStruct((N1 + NC, B), BF16), jax.ShapeDtypeStruct((N2, B), BF16)),
        grid_spec=pltpu.PrefetchScalarGridSpec(
            num_scalar_prefetch=1, grid=(), in_specs=[vmem] * 3, out_specs=[vmem] * 2,
        ),
    )(sector_rows, psi_blocks, connect, swap(connect))

    mytiles = lax.dynamic_slice_in_dim(tile_order, sec * TILES, TILES)
    lane = jnp.arange(B)[None, :]
    mypairs = jnp.pad(mytiles // 2, (0, 16 - TILES))[:, None]
    pick = jnp.where(lane == mypairs, 16.0, 0.0) + jnp.where(lane == B // 2 + mypairs, 1.0, 0.0)
    pick = pick.astype(BF16)

    index, places, segs = (jnp.asarray(t)[core] for t in tables())

    def slot_of(t):
        return (zpos + t[:, 0]) % NZ * NY + (ypos + t[:, 1]) % NY

    places = slot_of(places) * SEC + places[:, 2]
    rows_to = slot_of(segs) * ROWS + segs[:, 2]
    meta = jnp.concatenate([mytiles, core[None], index, places, rows_to]).astype(jnp.int32)
    couples, (meta, pick, ops) = gather_pieces(first, second, core, meta, pick, left_ops[mytiles // 2])

    arrays = arrays_of(couples)
    plan = [(segments, number) for _, segments, _, number in arrays]
    hbm = pl.BlockSpec(memory_space=pltpu.HBM)
    tiles = pl.pallas_call(
        functools.partial(tiles_kernel, [couple_spec(couple) for couple in couples], plan),
        out_shape=jax.ShapeDtypeStruct((TILES, 64, B), F32),
        grid_spec=pltpu.PrefetchScalarGridSpec(
            num_scalar_prefetch=1,
            grid=(),
            in_specs=[hbm] * len(plan) + [vmem, vmem],
            out_specs=vmem,
            scratch_shapes=[
                pltpu.VMEM((SLOTS * ROWS, B), BF16),
                pltpu.VMEM((TILES, SLOTS * SEC // 2, 64, 2 * B), BF16),
                pltpu.VMEM((TILES, 16, 64, 2 * B), BF16),
                pltpu.VMEM((SLOTS, 16, B), BF16),
                pltpu.VMEM((16, SLOTS * 16), jnp.int32),
                pltpu.SMEM((16, SLOTS * 16), jnp.int32),
                pltpu.SemaphoreType.DMA((len(couples),)),
                pltpu.SemaphoreType.DMA,
            ],
        ),
        compiler_params=pltpu.CompilerParams(vmem_limit_bytes=VMEM_LIMIT),
    )(meta, *[w for w, _, _, _ in arrays], ops, pick)
    ring = [((i - 1) % 8, i) for i in range(8)]
    return tiles + lax.ppermute(tiles, "pair", ring)


def solution(mesh):
    in_specs = (P("sec", None, None), P("sec"), P("pair", None, None), P("pair", "sec"), P())
    out_specs = P(("pair", "sec"), None, None)
    return jax.shard_map(
        per_device, mesh=mesh, in_specs=in_specs, out_specs=out_specs, check_vma=False
    )
```

```python
import functools

import jax
import jax.numpy as jnp
import numpy as np
from jax import lax
from jax.experimental import pallas as pl
from jax.experimental.pallas import tpu as pltpu
from jax.sharding import PartitionSpec as P

NZ, NY = 8, 4
SLOTS = NZ * NY
SEC = 12
B = 128
ROWS = SEC * B
S1 = 4
N1, N2 = S1 * B, (SEC - S1) * B
NC = 32
TILES = 3
VMEM_LIMIT = 60 * 2**20
AHEAD = 2
F32, BF16 = jnp.float32, jnp.bfloat16


def hop(v, dz, dy):
    route = []
    for pair in range(8):
        s = -1 if pair % 2 else 1
        for z in range(NZ):
            for y in range(NY):
                to = (z + s * dz) % NZ * NY + (y + s * dy) % NY
                route.append((pair * SLOTS + z * NY + y, pair * SLOTS + to))
    return lax.ppermute(v, ("pair", "sec"), route)


def zhop(v):
    return hop(v, 1, 0)


def yhop(v):
    return hop(v, 0, 1)


def swap(v):
    return lax.ppermute(v, "pair", [(i, i ^ 1) for i in range(lax.axis_size("pair"))])


def part(v, core, axis=0):
    n = v.shape[axis] // 2
    return lax.dynamic_slice_in_dim(v, core * n, n, axis)


YS = (0, 1, 2, -1)


def sync(*arrays):
    return lax.optimization_barrier(arrays)


def gather_pieces(first, second, core, *others):
    n, h2 = first.shape[0], N2 // 2
    w1, near, far = zhop(second), yhop(first), hop(part(first, core), 0, 2)
    w1, near, far, *others = sync(w1, near, far, *others)

    w2, other = zhop(w1), swap(jnp.concatenate([near, far, w1]))
    w2, other = sync(w2, other)

    near_s, far_s, w1s = other[:n], other[n:n + n // 2], other[n + n // 2:]
    far = jnp.where(core == 0, jnp.concatenate([far, far_s]), jnp.concatenate([far_s, far]))
    bundle = jnp.concatenate([first, near, far, near_s])
    own = jnp.where(core == 0, second, jnp.concatenate([second[h2:], second[:h2]]))
    a = jnp.concatenate([w1, own, w1s])
    w3, z1, a1 = zhop(w2), zhop(bundle), yhop(a)
    w4, w2s = hop(part(w2, core), 2, 0), swap(w2)
    w3, z1, a1, w4, w2s = sync(w3, z1, a1, w4, w2s)

    ha = a.shape[0] // 2
    b = jnp.concatenate([w2, w2s])
    wc = jnp.concatenate([w3, w4])
    z2, ab, wcs, a1s = zhop(z1), yhop(jnp.concatenate([a1[:ha], b])), swap(wc), swap(a1)
    z2, ab, wcs, a1s, b = sync(z2, ab, wcs, a1s, b)

    c = jnp.concatenate([wc, wcs])
    hb, hc = b.shape[0] // 2, c.shape[0] // 2
    z3, cb, z1s, abs_ = zhop(z2), yhop(jnp.concatenate([c, ab[ha:ha + hb]])), swap(z1), swap(ab)
    z3, cb, z1s, abs_, c = sync(z3, cb, z1s, abs_, c)

    z4, c2 = zhop(lax.dynamic_slice_in_dim(z3, core * n, 2 * n, 0)), yhop(cb[:hc])
    z2s, z3s, cbs = swap(z2), swap(z3), swap(cb)
    z4, c2, z2s, z3s, cbs = sync(z4, c2, z2s, z3s, cbs)
    z4s, c2s = swap(z4), swap(c2)

    def step(dz):
        return [(i * n, N1, dz, dy, 0, 0, False) for i, dy in enumerate(YS)]

    def shift(seg, dy, stop, by=0):
        return [(r + by, m, dz, dy, o, e, x) for r, m, dz, _, o, e, x in seg if r < stop]

    def rest(parts):
        segs, r = [], 0
        for rows, dz, o, more in parts:
            segs.append((r, rows, dz, 0, N1 + o, more, False))
            r += rows
        return segs

    a_seg = rest([(N2, 1, 0, 0), (h2, 0, 0, h2), (h2, 0, h2, -h2), (N2, -1, 0, 0)])
    b_seg = rest([(N2, 2, 0, 0), (N2, -2, 0, 0)])
    c_seg = rest([(N2, 3, 0, 0), (h2, 4, 0, h2), (N2, -3, 0, 0), (h2, 4, h2, -h2)])
    couples = [
        (bundle, None, step(0)), (a, None, a_seg), (z1, z1s, step(1)), (z2, z2s, step(2)),
        (z3, z3s, step(3)), (z4, z4s, [(i * n, N1, 4, i, 0, 0, True) for i in range(2)]),
        (a1, a1s, shift(a_seg, 1, 2 * ha)), (b, None, b_seg), (c, None, c_seg),
        (ab, abs_, shift(a_seg, 2, ha) + shift(b_seg, 1, 2 * hb, ha)),
        (cb, cbs, shift(c_seg, 1, 2 * hc) + shift(b_seg, 2, hb, 2 * hc)),
        (c2, c2s, shift(c_seg, 2, hc)),
    ]
    return couples, others


def place(seg, core, swapped):
    who = 1 - core if swapped else core
    sign = 2 * who - 1
    _, _, dz, dy, row, more, last = seg
    return dz * sign, (1 + dy if who else -dy) if last else dy * sign, row + more * who


def sectors(segments, core, swapped):
    found = []
    for seg in segments:
        dz, dy, row = place(seg, core, swapped)
        found += [(dz % NZ, dy % NY, row // B + q) for q in range(seg[1] // B)]
    return found


def arrays_of(couples):
    return [(w, seg, swapped, number) for number, (u, v, seg) in enumerate(couples)
            for w, swapped in ((u, False), (v, True)) if w is not None]


def couple_spec(couple):
    _, v, segments = couple
    count = sum(seg[1] for seg in segments) // B // (2 if v is None else 1)
    return count, next(n for n in (12, 16, 14, 8) if count % n == 0)


def tables():
    shapes = []

    def trace(first, second):
        couples, _ = gather_pieces(first, second, jnp.int32(0))
        shapes.extend(couples)
        return first

    jax.eval_shape(
        trace, jax.ShapeDtypeStruct((N1 + NC, B), BF16), jax.ShapeDtypeStruct((N2, B), BF16))
    index, names, rows = [], [], []
    for core in (0, 1):
        number = {}
        for _, segments, swapped, _ in arrays_of(shapes):
            for seg in segments:
                dz, dy, row = place(seg, core, swapped)
                if row < N1:
                    number[dz % NZ, dy % NY] = len(number)
        flat, held, base = [], [], 0
        for u, v, segments in shapes:
            sides = []
            for w, swapped in ((u, False), (v, True)):
                if w is not None:
                    at = [base + seg[0] + q * B for seg in segments for q in range(seg[1] // B)]
                    sides.append(list(zip(sectors(segments, core, swapped), at)))
                    base += w.shape[0]
            if v is None:
                half = len(sides[0]) // 2
                sides = [sides[0][:half], sides[0][half:]]
            for p in zip(*sides):
                flat += [t for t, _ in p]
                held += [at for _, at in p]
        index.append([number[t[:2]] * 16 + t[2] for t in flat])
        names.append(flat)
        rows.append(held)
    return (np.array(t, np.int32) for t in (index, names, rows))


def prepare_kernel(rows, psi, here, there, first, second):
    core = lax.rem(lax.axis_index("pair"), 2)
    row = lax.broadcasted_iota(jnp.int32, (B, B), 0)
    for s in range(SEC):
        live = jnp.where(row < rows[s], psi[s], jnp.zeros((B, B), BF16))
        if s < S1:
            first[pl.ds(s * B, B), :] = live
        else:
            second[pl.ds((s - S1) * B, B), :] = live
    pairs = here.shape[0]
    lane = lax.broadcasted_iota(jnp.int32, (pairs, B), 1)
    pair = lax.broadcasted_iota(jnp.int32, (pairs, B), 0)
    high = jnp.where(lane == pair, 1.0, 0.0).astype(BF16)
    low = jnp.where(lane == pair + B // 2, 1.0, 0.0).astype(BF16)

    def words(ref):
        v = ref[...]
        contract = (((0,), (0,)), ((), ()))
        up = (v // 16).astype(F32).astype(BF16)
        down = (v % 16).astype(F32).astype(BF16)
        return (lax.dot_general(up, high, contract, preferred_element_type=F32)
                + lax.dot_general(down, low, contract, preferred_element_type=F32)).astype(BF16)

    mine, other = words(here), words(there)
    zero = jnp.zeros((16 - SEC, B), BF16)
    even = jnp.where(core == 0, mine, other)
    odd = jnp.where(core == 0, other, mine)
    first[pl.ds(N1, NC), :] = jnp.concatenate([even, zero, odd, zero], axis=0)


def tiles_kernel(specs, plan, meta, *refs):
    n = len(plan)
    pieces, ops, pick, out = refs[:n], *refs[n:n + 3]
    psi, halves, turned, table, conn, sems, csem = refs[n + 3:]
    core = meta[TILES]
    pairs = SLOTS * SEC // 2
    targets, places, row_of = TILES + 1, TILES + 1 + 2 * pairs, TILES + 1 + 4 * pairs
    size = [sum(ref.shape[0] for ref, (_, c) in zip(pieces, plan) if c == couple) for couple in range(len(specs))]

    def fetch(wanted):
        base = 0
        for ref, (_, couple) in zip(pieces, plan):
            if couple == wanted:
                to = psi.at[pl.ds(base, ref.shape[0])]
                pltpu.make_async_copy(ref, to, sems.at[couple]).start()
            base += ref.shape[0]

    for couple in range(AHEAD):
        fetch(couple)

    def read_connect():
        words, base = [], 0
        for ref, (segments, _) in zip(pieces, plan):
            for r, _, _, _, row, _, _ in segments:
                if row < N1:
                    words.append(psi[pl.ds(pl.multiple_of(base + r + N1 + core * 16, 16), 16), :])
            base += ref.shape[0]
        values = lax.dot_general(pick[...], jnp.concatenate(words, axis=0), (((1,), (1,)), ((), ())),
                                 preferred_element_type=F32)
        table[...] = values.astype(jnp.int32)
        pltpu.make_async_copy(table, conn, csem).start()

    def sector(s):
        return psi[pl.ds(pl.multiple_of(s, 32), B), :]

    base = 0
    for couple, (count, batch) in enumerate(specs):
        fetch(couple + AHEAD)
        rows = psi.at[pl.ds(0, size[couple])]
        pltpu.make_async_copy(rows, rows, sems.at[couple]).wait()

        def some(j, carry, batch=batch, base=base):
            for q in range(batch):
                for e in range(2):
                    t = sector(meta[places + 2 * (base + j * batch + q) + e]).T
                    for k in range(TILES):
                        low = lax.rem(meta[k], 2) == 0
                        turned[k, q, :, pl.ds(e * B, B)] = jnp.where(low, t[:64], t[64:])
            for k in range(TILES):
                for e in range(2):
                    rows = turned[k, pl.ds(0, batch), :, pl.ds(e * B, B)].reshape(batch * 64, B)
                    r = jnp.dot(rows, ops[k], preferred_element_type=F32).astype(BF16)
                    to = pl.ds(base + j * batch, batch)
                    halves[k, to, :, pl.ds(e * B, B)] = r.reshape(batch, 64, B)
            return carry

        lax.fori_loop(0, count // batch, some, 0)
        base += count
        if couple == 5:
            read_connect()
    pltpu.make_async_copy(table, conn, csem).wait()

    unroll = 48

    def second_stage(j, sums):
        sums = list(sums)
        for u in range(unroll):
            at = j * unroll + u
            for k in range(TILES):
                left, right = (meta[row_of + conn[k, meta[targets + 2 * at + e]]] for e in (0, 1))
                rhs = jnp.concatenate([sector(left), sector(right)], axis=0)
                sums[k] = sums[k] + jnp.dot(halves[k, at], rhs, preferred_element_type=F32)
        return tuple(sums)

    sums = lax.fori_loop(0, pairs // unroll, second_stage, (jnp.zeros((64, B), F32),) * TILES)
    for k in range(TILES):
        out[k] = sums[k]


def per_device(psi_blocks, sector_rows, left_ops, connect, tile_order):
    sec, pair = lax.axis_index("sec"), lax.axis_index("pair")
    zpos, ypos, core = sec // NY, sec % NY, pair % 2
    vmem = pl.BlockSpec(memory_space=pltpu.VMEM)
    first, second = pl.pallas_call(
        prepare_kernel,
        out_shape=(jax.ShapeDtypeStruct((N1 + NC, B), BF16), jax.ShapeDtypeStruct((N2, B), BF16)),
        grid_spec=pltpu.PrefetchScalarGridSpec(
            num_scalar_prefetch=1, grid=(), in_specs=[vmem] * 3, out_specs=[vmem] * 2,
        ),
    )(sector_rows, psi_blocks, connect, swap(connect))

    mytiles = lax.dynamic_slice_in_dim(tile_order, sec * TILES, TILES)
    lane = jnp.arange(B)[None, :]
    mypairs = jnp.pad(mytiles // 2, (0, 16 - TILES))[:, None]
    pick = jnp.where(lane == mypairs, 16.0, 0.0) + jnp.where(lane == B // 2 + mypairs, 1.0, 0.0)
    pick = pick.astype(BF16)

    index, names, rows = (jnp.asarray(t)[core] for t in tables())
    slot = (zpos + names[:, 0]) % NZ * NY + (ypos + names[:, 1]) % NY
    here = (slot * SEC + names[:, 2])[None, :] == jnp.arange(SLOTS * SEC)[:, None]
    row_of = jnp.sum(jnp.where(here, rows[None, :], 0), axis=1)
    meta = jnp.concatenate([mytiles, core[None], index, rows, row_of]).astype(jnp.int32)
    couples, (meta, pick, ops) = gather_pieces(first, second, core, meta, pick, left_ops[mytiles // 2])

    arrays = arrays_of(couples)
    plan = [(segments, number) for _, segments, _, number in arrays]
    hbm = pl.BlockSpec(memory_space=pltpu.HBM)
    tiles = pl.pallas_call(
        functools.partial(tiles_kernel, [couple_spec(couple) for couple in couples], plan),
        out_shape=jax.ShapeDtypeStruct((TILES, 64, B), F32),
        grid_spec=pltpu.PrefetchScalarGridSpec(
            num_scalar_prefetch=1,
            grid=(),
            in_specs=[hbm] * len(plan) + [vmem, vmem],
            out_specs=vmem,
            scratch_shapes=[
                pltpu.VMEM((SLOTS * (ROWS + NC), B), BF16),
                pltpu.VMEM((TILES, SLOTS * SEC // 2, 64, 2 * B), BF16),
                pltpu.VMEM((TILES, 16, 64, 2 * B), BF16),
                pltpu.VMEM((16, SLOTS * 16), jnp.int32),
                pltpu.SMEM((16, SLOTS * 16), jnp.int32),
                pltpu.SemaphoreType.DMA((len(couples),)),
                pltpu.SemaphoreType.DMA,
            ],
        ),
        compiler_params=pltpu.CompilerParams(vmem_limit_bytes=VMEM_LIMIT),
    )(meta, *[w for w, _, _, _ in arrays], ops, pick)
    ring = [((i - 1) % 8, i) for i in range(8)]
    return tiles + lax.ppermute(tiles, "pair", ring)


def solution(mesh):
    in_specs = (P("sec", None, None), P("sec"), P("pair", None, None), P("pair", "sec"), P())
    out_specs = P(("pair", "sec"), None, None)
    return jax.shard_map(
        per_device, mesh=mesh, in_specs=in_specs, out_specs=out_specs, check_vma=False
    )
```

```python
import functools

import jax
import jax.numpy as jnp
import numpy as np
from jax import lax
from jax.experimental import pallas as pl
from jax.experimental.pallas import tpu as pltpu
from jax.sharding import PartitionSpec as P

NZ, NY = 8, 4
SLOTS = NZ * NY
SEC = 12
B = 128
ROWS = SEC * B
S1 = 4
N1, N2 = S1 * B, (SEC - S1) * B
NC = 32
TILES = 3
VMEM_LIMIT = 60 * 2**20
AHEAD = 4
F32, BF16 = jnp.float32, jnp.bfloat16


def hop(v, dz, dy):
    route = []
    for pair in range(8):
        s = -1 if pair % 2 else 1
        for z in range(NZ):
            for y in range(NY):
                to = (z + s * dz) % NZ * NY + (y + s * dy) % NY
                route.append((pair * SLOTS + z * NY + y, pair * SLOTS + to))
    return lax.ppermute(v, ("pair", "sec"), route)


def zhop(v):
    return hop(v, 1, 0)


def yhop(v):
    return hop(v, 0, 1)


def swap(v):
    return lax.ppermute(v, "pair", [(i, i ^ 1) for i in range(lax.axis_size("pair"))])


def part(v, core, axis=0):
    n = v.shape[axis] // 2
    return lax.dynamic_slice_in_dim(v, core * n, n, axis)


YS = (0, 1, 2, -1)


def sync(*arrays):
    return lax.optimization_barrier(arrays)


def gather_pieces(first, second, core, *others):
    n, h2 = first.shape[0], N2 // 2
    w1, near, far = zhop(second), yhop(first), hop(part(first, core), 0, 2)
    w1, near, far, *others = sync(w1, near, far, *others)

    w2, other = zhop(w1), swap(jnp.concatenate([near, far, w1]))
    w2, other = sync(w2, other)

    near_s, far_s, w1s = other[:n], other[n:n + n // 2], other[n + n // 2:]
    far = jnp.where(core == 0, jnp.concatenate([far, far_s]), jnp.concatenate([far_s, far]))
    bundle = jnp.concatenate([first, near, far, near_s])
    own = jnp.where(core == 0, second, jnp.concatenate([second[h2:], second[:h2]]))
    a = jnp.concatenate([w1, own, w1s])
    w3, z1, a1 = zhop(w2), zhop(bundle), yhop(a)
    w4, w2s = hop(part(w2, core), 2, 0), swap(w2)
    w3, z1, a1, w4, w2s = sync(w3, z1, a1, w4, w2s)

    ha = a.shape[0] // 2
    b = jnp.concatenate([w2, w2s])
    wc = jnp.concatenate([w3, w4])
    z2, ab, wcs, a1s = zhop(z1), yhop(jnp.concatenate([a1[:ha], b])), swap(wc), swap(a1)
    z2, ab, wcs, a1s, b = sync(z2, ab, wcs, a1s, b)

    c = jnp.concatenate([wc, wcs])
    hb, hc = b.shape[0] // 2, c.shape[0] // 2
    z3, cb, z1s, abs_ = zhop(z2), yhop(jnp.concatenate([c, ab[ha:ha + hb]])), swap(z1), swap(ab)
    z3, cb, z1s, abs_, c = sync(z3, cb, z1s, abs_, c)

    z4, c2 = zhop(lax.dynamic_slice_in_dim(z3, core * n, 2 * n, 0)), yhop(cb[:hc])
    z2s, z3s, cbs = swap(z2), swap(z3), swap(cb)
    z4, c2, z2s, z3s, cbs = sync(z4, c2, z2s, z3s, cbs)
    z4s, c2s = swap(z4), swap(c2)

    def step(dz):
        return [(i * n, N1, dz, dy, 0, 0, False) for i, dy in enumerate(YS)]

    def shift(seg, dy, stop, by=0):
        return [(r + by, m, dz, dy, o, e, x) for r, m, dz, _, o, e, x in seg if r < stop]

    def rest(parts):
        segs, r = [], 0
        for rows, dz, o, more in parts:
            segs.append((r, rows, dz, 0, N1 + o, more, False))
            r += rows
        return segs

    a_seg = rest([(N2, 1, 0, 0), (h2, 0, 0, h2), (h2, 0, h2, -h2), (N2, -1, 0, 0)])
    b_seg = rest([(N2, 2, 0, 0), (N2, -2, 0, 0)])
    c_seg = rest([(N2, 3, 0, 0), (h2, 4, 0, h2), (N2, -3, 0, 0), (h2, 4, h2, -h2)])
    couples = [
        (bundle, None, step(0)), (a, None, a_seg), (z1, z1s, step(1)), (z2, z2s, step(2)),
        (z3, z3s, step(3)), (z4, z4s, [(i * n, N1, 4, i, 0, 0, True) for i in range(2)]),
        (a1, a1s, shift(a_seg, 1, 2 * ha)), (b, None, b_seg), (c, None, c_seg),
        (ab, abs_, shift(a_seg, 2, ha) + shift(b_seg, 1, 2 * hb, ha)),
        (cb, cbs, shift(c_seg, 1, 2 * hc) + shift(b_seg, 2, hb, 2 * hc)),
        (c2, c2s, shift(c_seg, 2, hc)),
    ]
    return couples, others


def place(seg, core, swapped):
    who = 1 - core if swapped else core
    sign = 2 * who - 1
    _, _, dz, dy, row, more, last = seg
    return dz * sign, (1 + dy if who else -dy) if last else dy * sign, row + more * who


def sectors(segments, core, swapped):
    found = []
    for seg in segments:
        dz, dy, row = place(seg, core, swapped)
        found += [(dz % NZ, dy % NY, row // B + q) for q in range(seg[1] // B)]
    return found


def arrays_of(couples):
    return [(w, seg, swapped, number) for number, (u, v, seg) in enumerate(couples)
            for w, swapped in ((u, False), (v, True)) if w is not None]


def couple_spec(couple):
    _, v, segments = couple
    count = sum(seg[1] for seg in segments) // B // (2 if v is None else 1)
    return count, next(n for n in (12, 16, 14, 8) if count % n == 0)


def tables():
    shapes = []

    def trace(first, second):
        couples, _ = gather_pieces(first, second, jnp.int32(0))
        shapes.extend(couples)
        return first

    jax.eval_shape(
        trace, jax.ShapeDtypeStruct((N1 + NC, B), BF16), jax.ShapeDtypeStruct((N2, B), BF16))
    index, names, rows = [], [], []
    for core in (0, 1):
        number = {}
        for _, segments, swapped, _ in arrays_of(shapes):
            for seg in segments:
                dz, dy, row = place(seg, core, swapped)
                if row < N1:
                    number[dz % NZ, dy % NY] = len(number)
        flat, held, base = [], [], 0
        for u, v, segments in shapes:
            sides = []
            for w, swapped in ((u, False), (v, True)):
                if w is not None:
                    at = [base + seg[0] + q * B for seg in segments for q in range(seg[1] // B)]
                    sides.append(list(zip(sectors(segments, core, swapped), at)))
                    base += w.shape[0]
            if v is None:
                half = len(sides[0]) // 2
                sides = [sides[0][:half], sides[0][half:]]
            for p in zip(*sides):
                flat += [t for t, _ in p]
                held += [at for _, at in p]
        index.append([number[t[:2]] * 16 + t[2] for t in flat])
        names.append(flat)
        rows.append(held)
    return (np.array(t, np.int32) for t in (index, names, rows))


def prepare_kernel(rows, psi, here, there, first, second):
    core = lax.rem(lax.axis_index("pair"), 2)
    row = lax.broadcasted_iota(jnp.int32, (B, B), 0)
    for s in range(SEC):
        live = jnp.where(row < rows[s], psi[s], jnp.zeros((B, B), BF16))
        if s < S1:
            first[pl.ds(s * B, B), :] = live
        else:
            second[pl.ds((s - S1) * B, B), :] = live
    pairs = here.shape[0]
    lane = lax.broadcasted_iota(jnp.int32, (pairs, B), 1)
    pair = lax.broadcasted_iota(jnp.int32, (pairs, B), 0)
    high = jnp.where(lane == pair, 1.0, 0.0).astype(BF16)
    low = jnp.where(lane == pair + B // 2, 1.0, 0.0).astype(BF16)

    def words(ref):
        v = ref[...]
        contract = (((0,), (0,)), ((), ()))
        up = (v // 16).astype(F32).astype(BF16)
        down = (v % 16).astype(F32).astype(BF16)
        return (lax.dot_general(up, high, contract, preferred_element_type=F32)
                + lax.dot_general(down, low, contract, preferred_element_type=F32)).astype(BF16)

    mine, other = words(here), words(there)
    zero = jnp.zeros((16 - SEC, B), BF16)
    even = jnp.where(core == 0, mine, other)
    odd = jnp.where(core == 0, other, mine)
    first[pl.ds(N1, NC), :] = jnp.concatenate([even, zero, odd, zero], axis=0)


def tiles_kernel(specs, plan, meta, *refs):
    n = len(plan)
    pieces, ops, pick, out = refs[:n], *refs[n:n + 3]
    psi, halves, turned, table, conn, sems, csem = refs[n + 3:]
    core = meta[TILES]
    pairs = SLOTS * SEC // 2
    targets, places, row_of = TILES + 1, TILES + 1 + 2 * pairs, TILES + 1 + 4 * pairs
    size = [sum(ref.shape[0] for ref, (_, c) in zip(pieces, plan) if c == couple) for couple in range(len(specs))]

    def fetch(wanted):
        base = 0
        for ref, (_, couple) in zip(pieces, plan):
            if couple == wanted:
                to = psi.at[pl.ds(base, ref.shape[0])]
                pltpu.make_async_copy(ref, to, sems.at[couple]).start()
            base += ref.shape[0]

    for couple in range(AHEAD):
        fetch(couple)

    def read_connect():
        words, base = [], 0
        for ref, (segments, _) in zip(pieces, plan):
            for r, _, _, _, row, _, _ in segments:
                if row < N1:
                    words.append(psi[pl.ds(pl.multiple_of(base + r + N1 + core * 16, 16), 16), :])
            base += ref.shape[0]
        values = lax.dot_general(pick[...], jnp.concatenate(words, axis=0), (((1,), (1,)), ((), ())),
                                 preferred_element_type=F32)
        table[...] = values.astype(jnp.int32)
        pltpu.make_async_copy(table, conn, csem).start()

    def sector(s):
        return psi[pl.ds(pl.multiple_of(s, 32), B), :]

    base = 0
    for couple, (count, batch) in enumerate(specs):
        fetch(couple + AHEAD)
        rows = psi.at[pl.ds(0, size[couple])]
        pltpu.make_async_copy(rows, rows, sems.at[couple]).wait()

        def some(j, carry, batch=batch, base=base):
            for q in range(batch):
                for e in range(2):
                    t = sector(meta[places + 2 * (base + j * batch + q) + e]).T
                    for k in range(TILES):
                        low = lax.rem(meta[k], 2) == 0
                        turned[k, q, :, pl.ds(e * B, B)] = jnp.where(low, t[:64], t[64:])
            for k in range(TILES):
                for e in range(2):
                    rows = turned[k, pl.ds(0, batch), :, pl.ds(e * B, B)].reshape(batch * 64, B)
                    r = jnp.dot(rows, ops[k], preferred_element_type=F32).astype(BF16)
                    to = pl.ds(base + j * batch, batch)
                    halves[k, to, :, pl.ds(e * B, B)] = r.reshape(batch, 64, B)
            return carry

        lax.fori_loop(0, count // batch, some, 0)
        base += count
        if couple == 5:
            read_connect()
    pltpu.make_async_copy(table, conn, csem).wait()

    unroll = 48

    def second_stage(j, sums):
        sums = list(sums)
        for u in range(unroll):
            at = j * unroll + u
            for k in range(TILES):
                left, right = (meta[row_of + conn[k, meta[targets + 2 * at + e]]] for e in (0, 1))
                rhs = jnp.concatenate([sector(left), sector(right)], axis=0)
                sums[k] = sums[k] + jnp.dot(halves[k, at], rhs, preferred_element_type=F32)
        return tuple(sums)

    sums = lax.fori_loop(0, pairs // unroll, second_stage, (jnp.zeros((64, B), F32),) * TILES)
    for k in range(TILES):
        out[k] = sums[k]


def per_device(psi_blocks, sector_rows, left_ops, connect, tile_order):
    sec, pair = lax.axis_index("sec"), lax.axis_index("pair")
    zpos, ypos, core = sec // NY, sec % NY, pair % 2
    vmem = pl.BlockSpec(memory_space=pltpu.VMEM)
    first, second = pl.pallas_call(
        prepare_kernel,
        out_shape=(jax.ShapeDtypeStruct((N1 + NC, B), BF16), jax.ShapeDtypeStruct((N2, B), BF16)),
        grid_spec=pltpu.PrefetchScalarGridSpec(
            num_scalar_prefetch=1, grid=(), in_specs=[vmem] * 3, out_specs=[vmem] * 2,
        ),
    )(sector_rows, psi_blocks, connect, swap(connect))

    mytiles = lax.dynamic_slice_in_dim(tile_order, sec * TILES, TILES)
    lane = jnp.arange(B)[None, :]
    mypairs = jnp.pad(mytiles // 2, (0, 16 - TILES))[:, None]
    pick = jnp.where(lane == mypairs, 16.0, 0.0) + jnp.where(lane == B // 2 + mypairs, 1.0, 0.0)
    pick = pick.astype(BF16)

    index, names, rows = (jnp.asarray(t)[core] for t in tables())
    slot = (zpos + names[:, 0]) % NZ * NY + (ypos + names[:, 1]) % NY
    here = (slot * SEC + names[:, 2])[None, :] == jnp.arange(SLOTS * SEC)[:, None]
    row_of = jnp.sum(jnp.where(here, rows[None, :], 0), axis=1)
    meta = jnp.concatenate([mytiles, core[None], index, rows, row_of]).astype(jnp.int32)
    couples, (meta, pick, ops) = gather_pieces(first, second, core, meta, pick, left_ops[mytiles // 2])

    arrays = arrays_of(couples)
    plan = [(segments, number) for _, segments, _, number in arrays]
    hbm = pl.BlockSpec(memory_space=pltpu.HBM)
    tiles = pl.pallas_call(
        functools.partial(tiles_kernel, [couple_spec(couple) for couple in couples], plan),
        out_shape=jax.ShapeDtypeStruct((TILES, 64, B), F32),
        grid_spec=pltpu.PrefetchScalarGridSpec(
            num_scalar_prefetch=1,
            grid=(),
            in_specs=[hbm] * len(plan) + [vmem, vmem],
            out_specs=vmem,
            scratch_shapes=[
                pltpu.VMEM((SLOTS * (ROWS + NC), B), BF16),
                pltpu.VMEM((TILES, SLOTS * SEC // 2, 64, 2 * B), BF16),
                pltpu.VMEM((TILES, 16, 64, 2 * B), BF16),
                pltpu.VMEM((16, SLOTS * 16), jnp.int32),
                pltpu.SMEM((16, SLOTS * 16), jnp.int32),
                pltpu.SemaphoreType.DMA((len(couples),)),
                pltpu.SemaphoreType.DMA,
            ],
        ),
        compiler_params=pltpu.CompilerParams(vmem_limit_bytes=VMEM_LIMIT),
    )(meta, *[w for w, _, _, _ in arrays], ops, pick)
    ring = [((i - 1) % 8, i) for i in range(8)]
    return tiles + lax.ppermute(tiles, "pair", ring)


def solution(mesh):
    in_specs = (P("sec", None, None), P("sec"), P("pair", None, None), P("pair", "sec"), P())
    out_specs = P(("pair", "sec"), None, None)
    return jax.shard_map(
        per_device, mesh=mesh, in_specs=in_specs, out_specs=out_specs, check_vma=False
    )
```
